32 devices in a mesh: row: 4 (over z), col: 8 (over y, x, core).
Axes of the slice: x: 2, y: 2, z: 4, core: 2. Of those that a mesh axis runs over, the one named last changes fastest.
Arguments:
- embeddings: bfloat16 [10240, 256], P(('row', 'col')), may hold values from -90 to 90
- start_vectors: float32 [32, 10240], P(None, ('row', 'col')), may hold values from -6 to 6
Outputs:
- vectors: float32 [32, 10240], P(None, ('row', 'col'))
- degrees: float32 [10240], P(('row', 'col'))
The draws below stay inside these ranges and needn't reach their ends.
All inputs are finite; a program needn't handle non-finite values.
Results may differ from the reference program's by a relative error of at most 0.015.
Values may be sent and summed in bfloat16 or wider, within the bound.
No kernel may reach another device: no remote copies, remote signals or barrier semaphores. Data moves between devices by JAX's collectives and lax.ppermute only.
A program may use at most 128 MiB of HBM per device.

```python
import jax
import jax.numpy as jnp
from jax import lax

E = 256
K = 32
ITERS = 2
SPEAKERS = 64
NSEG = 10240
ROW_BLOCK = 2560


def draw_embeddings(key, part):
    key = jax.random.fold_in(key, 11)
    label_key, centre_key, strength_key, noise_key = jax.random.split(key, 4)
    labels = jax.random.randint(label_key, (NSEG,), 0, SPEAKERS)
    centres = jnp.clip(jax.random.normal(centre_key, (SPEAKERS, E), jnp.float32), -4.0, 4.0)
    strength = jax.random.uniform(strength_key, (NSEG, 1), jnp.float32, 0.6, 1.4)
    noise = 0.8 * jnp.clip(jax.random.normal(noise_key, (NSEG, E), jnp.float32), -4.0, 4.0)
    values = strength * jnp.take(centres, labels, axis=0) + noise
    return values.astype(jnp.bfloat16)


def block_levels(stream_key, shape, shards, least, top_value):
    def one(position, blocks):
        steps = jax.random.uniform(jax.random.fold_in(jax.random.fold_in(stream_key, 6), position), (blocks,), jnp.float32, least / len(shards), top_value / len(shards))
        return jnp.repeat(jnp.exp(steps), shape[position] // blocks).reshape((-1,) + (1,) * (len(shape) - position - 1))

    gain = one(*shards[0])
    for cut in shards[1:]:
        gain = gain * one(*cut)
    return gain


def normal_values(key, shape, spread, limit, cuts=(), kind=jnp.bfloat16):
    level = block_levels(key, shape, cuts, -0.22, 0.18) if cuts else 1.0
    result = jax.random.normal(key, shape, jnp.float32) * spread * level
    return jnp.minimum(jnp.maximum(result, -limit), limit).astype(kind)


def setup_inputs(seed: int = 0) -> dict:
    key_list = jax.random.split(jax.random.key(seed), 3)
    return {
        "embeddings": draw_embeddings(jax.random.fold_in(key_list[2], 71), 0),
        "start_vectors": normal_values(key_list[1], (K, NSEG), 1.0, 6.0, ((1, 32),), jnp.float32),
    }


def normalize(embeddings):
    values = embeddings.astype(jnp.float32)
    power = lax.optimization_barrier(jnp.mean(values * values, axis=1, keepdims=True))
    return (values * lax.rsqrt(power + 1e-06) / jnp.sqrt(jnp.float32(E))).astype(jnp.bfloat16)

def affinity_block(left, right):
    inner = jnp.dot(left.astype(jnp.float32), right.astype(jnp.float32).T, precision=lax.Precision.HIGHEST)
    return jnp.exp(8.0 * (inner - 1.0)).astype(jnp.bfloat16)

def reference(embeddings, start_vectors):
    unit = normalize(embeddings)
    blocks = NSEG // ROW_BLOCK
    unit_blocks = unit.reshape(blocks, ROW_BLOCK, E)

    def degree_of(block):
        return lax.optimization_barrier(jnp.sum(affinity_block(block, unit).astype(jnp.float32), axis=1))
    degrees = lax.map(degree_of, unit_blocks).reshape(NSEG)
    scale = 1.0 / jnp.sqrt(degrees)
    current = start_vectors
    for step in range(ITERS):
        scaled = (current * scale[None, :]).astype(jnp.bfloat16).astype(jnp.float32)

        def apply_block(block):
            tile = affinity_block(block, unit).astype(jnp.float32)
            return jnp.dot(scaled, tile.T, precision=lax.Precision.HIGHEST)
        image = lax.map(apply_block, unit_blocks)
        image = jnp.transpose(image, (1, 0, 2)).reshape(K, NSEG) * scale[None, :]
        gram = jnp.dot(image, image.T, precision=lax.Precision.HIGHEST)
        lower = jnp.linalg.cholesky(gram)
        current = lax.linalg.triangular_solve(lower, image, left_side=True, lower=True)
    return (current, degrees)
```

```python
import functools
import math

import jax
import jax.numpy as jnp
from jax import lax
from jax.experimental import pallas as pl
from jax.experimental.pallas import tpu as pltpu
from jax.sharding import PartitionSpec as P

VMEM = pl.BlockSpec(memory_space=pltpu.VMEM)
NT = (((1,), (1,)), ((), ()))
HIGH = lax.Precision.HIGHEST


def lanes(width):
    return -(-width // 128) * 128


def call(kernel, out_shapes, scratch=(), flops=0):
    count = len(out_shapes)
    mib = 1024 * 1024

    def run(*operands):
        needs = sum(math.prod(o.shape) * jnp.dtype(o.dtype).itemsize for o in operands)
        needs += sum(math.prod(s) * jnp.dtype(d).itemsize for s, d in out_shapes)
        limit = min(56 * mib, 2 * needs // mib * mib + 8 * mib)
        return pl.pallas_call(
            kernel,
            out_shape=[jax.ShapeDtypeStruct(s, d) for s, d in out_shapes],
            in_specs=[VMEM] * len(operands),
            out_specs=[VMEM] * count,
            scratch_shapes=list(scratch),
            compiler_params=pltpu.CompilerParams(vmem_limit_bytes=limit),
            cost_estimate=pl.CostEstimate(flops=flops, bytes_accessed=0, transcendentals=0),
        )(*operands)

    return run


def side_by_side(blocks):
    return jnp.concatenate(blocks, axis=1) if len(blocks) > 1 else blocks[0]


def cut(value, width):
    return [value[:, i : i + width] for i in range(0, value.shape[1], width)]


def two_parts(value):
    high = value.astype(jnp.bfloat16)
    return high, (value - high.astype(jnp.float32)).astype(jnp.bfloat16)


def unit_rows(ref, gain):
    values = ref[...].astype(jnp.float32)
    power = jnp.mean(values * values, axis=1, keepdims=True)
    factor = lax.rsqrt(power + 1e-06) * (gain / math.sqrt(ref.shape[1]))
    return (values * factor).astype(jnp.bfloat16)


def own_kernel(emb_ref, start_ref, unit_ref, out_ref):
    unit_ref[...] = unit_rows(emb_ref, 1.0)
    out_ref[...] = start_ref[...].astype(out_ref.dtype)


def affinity(rows_ref, parts, own, fold_ref, more_ref=None):
    def row_block(start):
        piece = rows_ref[pl.ds(start, own), :]
        fold = 0.0 if more_ref is None else more_ref[pl.ds(start, own), :]
        for lanes_ref, first, tile_ref in parts:
            total = tile_ref.shape[1]
            for j in range(0, total, 256):
                stop = min(j + 256, total)
                inner = lax.dot_general(
                    piece, lanes_ref[first + j : first + stop, :], NT,
                    preferred_element_type=jnp.float32,
                )
                values = jnp.exp(inner - 8.0)
                tile_ref[pl.ds(start, own), j:stop] = values.astype(jnp.bfloat16)
                for part in cut(values, 128):
                    gap = 128 - part.shape[1]
                    if gap:
                        part = side_by_side([part, jnp.zeros((own, gap), jnp.float32)])
                    fold = fold + part
        fold_ref[pl.ds(start, own), :] = fold

    count = rows_ref.shape[0] // own
    if count <= 4:
        for i in range(count):
            row_block(i * own)
    else:
        pl.loop(0, count)(lambda i: row_block(pl.multiple_of(i * own, own)))


def unfold(fold):
    ones = jnp.ones((8, fold.shape[1]), jnp.float32)
    sums = lax.dot_general(ones, fold, NT, precision=HIGH, preferred_element_type=jnp.float32)
    return sums[0:1, :]


def main_kernel(rows, unit_ref, *refs):
    row_refs, lane_refs = refs[: rows - 1], refs[rows - 1 : -6]
    rows_ref, even_ref, odd_ref, even_tile_ref, odd_tile_ref, fold_ref = refs[-6:]
    own = unit_ref.shape[0]
    rows_ref[0:own, :] = unit_ref[...] * 8
    even_ref[0:own, :] = unit_ref[...]
    for i, ref in enumerate(row_refs, 1):
        rows_ref[i * own : (i + 1) * own, :] = unit_rows(ref, 8.0)
    half = (len(lane_refs) + 1) // 2
    for i, ref in enumerate(lane_refs, 1):
        target, at = (even_ref, i) if i < half else (odd_ref, i - half)
        target[at * own : (at + 1) * own, :] = unit_rows(ref, 1.0)
    parts = [(even_ref, 0, even_tile_ref), (odd_ref, 0, odd_tile_ref)]
    affinity(rows_ref, parts, own, fold_ref)


def rest_kernel(rows_ref, fold_in_ref, even_in_ref, odd_in_ref, *refs):
    row_ref, even_ref, odd_ref, start_ref = refs[:4]
    side_tile_ref, even_last_ref, odd_last_ref, sums_ref, send_ref = refs[4:9]
    last_ref, even_all, odd_all, side_all, fold_ref, fold_last_ref = refs[9:]
    own = row_ref.shape[0]
    high = even_in_ref.shape[0]
    sides = ((even_in_ref, even_ref, even_all), (odd_in_ref, odd_ref, odd_all))
    for i, (before, fresh, whole) in enumerate(sides):
        unit = unit_rows(fresh, 1.0)
        whole[0:high, :] = before[...]
        whole[high : high + own, :] = unit
        side_all[i * own : (i + 1) * own, :] = unit
    affinity(rows_ref, [(side_all, 0, side_tile_ref)], own, fold_ref, fold_in_ref)
    last_ref[...] = unit_rows(row_ref, 8.0)
    parts = [(even_all, 0, even_last_ref), (odd_all, 0, odd_last_ref)]
    affinity(last_ref, parts, own, fold_last_ref)
    lines = cut(unfold(fold_ref[...]), own) + [unfold(fold_last_ref[...])]
    sums = jnp.concatenate(lines, axis=0)
    sums_ref[...] = sums
    parts = [start_ref[...].astype(jnp.float32)]
    parts += [part.astype(jnp.float32) for part in two_parts(sums)]
    space = send_ref.shape[0] - sum(p.shape[0] for p in parts)
    if space:
        parts.append(jnp.zeros((space, own), jnp.float32))
    send_ref[...] = jnp.concatenate(parts, axis=0).astype(jnp.bfloat16)


def side_span(odd, own):
    low = own // 128 * 128 if odd else 0
    return low, (2 * own if odd else lanes(own)), odd * own - low


def lane_products(left, last, tiles, odd, own):
    main_ref, side_ref, last_ref = tiles

    def product(value, ref, low, high):
        return side_by_side(
            [
                jnp.dot(value, ref[:, i : min(i + 256, high)], preferred_element_type=jnp.float32)
                for i in range(low, high, 256)
            ]
        )

    low, high, at = side_span(odd, own)
    blocks = cut(product(left, main_ref, 0, main_ref.shape[1]), own)
    blocks.append(product(left, side_ref, low, high)[:, at : at + own])
    more = cut(product(last, last_ref, 0, last_ref.shape[1]), own)
    return [x + y for x, y in zip(blocks, more)]


def with_tail(block, tail, width):
    space = width - block.shape[1] - tail.shape[1]
    parts = [block, tail]
    if space:
        parts.append(jnp.zeros((block.shape[0], space), jnp.float32))
    return side_by_side(parts)


def gram_tail(gram):
    return side_by_side([p.astype(jnp.float32) for p in two_parts(gram)])


def gram_of(piece, own):
    count = piece.shape[0]
    return piece[:, own : own + count] + piece[:, own + count : own + 2 * count]


def scale_tail(scale, count, space):
    lines = []
    for part in two_parts(scale):
        for piece in cut(part.astype(jnp.float32), space):
            gap = space - piece.shape[1]
            lines.append(side_by_side([piece, jnp.zeros((1, gap), jnp.float32)]) if gap else piece)
    lines.append(jnp.zeros((count - len(lines), space), jnp.float32))
    return jnp.concatenate(lines, axis=0)


def scale_of(tail, own):
    lines = -(-own // tail.shape[1])
    parts = [
        side_by_side([tail[k + i : k + i + 1] for i in range(lines)])[:, :own]
        for k in (0, lines)
    ]
    return parts[0] + parts[1]


def first_kernel(*refs):
    tiles, refs = refs[:3], refs[3:]
    sums_ref, start_ref, came_refs = refs[0], refs[1], refs[2:-5]
    pieces_ref, left_ref, left_last_ref, degrees_ref, scale_ref = refs[-5:]
    count, own = start_ref.shape
    rows = sums_ref.shape[0]
    sums, starts = [sums_ref[...]], [start_ref[...].astype(jnp.float32)]
    for ref in came_refs:
        came = ref[...].astype(jnp.float32)
        starts.append(came[:count])
        high, low = (came[count + i * rows : count + (i + 1) * rows] for i in range(2))
        sums.append(high + low)
    degrees = []
    for j in range(rows):
        degrees.append(sum(s[j ^ m : (j ^ m) + 1, :] for m, s in enumerate(sums)))
    degrees_ref[...] = degrees[0]
    scales = [1.0 / jnp.sqrt(d) for d in degrees]
    scale_ref[...] = scales[0]
    scaled = [(start * scale).astype(jnp.bfloat16) for start, scale in zip(starts, scales)]
    left_ref[...] = side_by_side(scaled[:-1])
    left_last_ref[...] = scaled[-1]
    blocks = lane_products(left_ref[...], left_last_ref[...], tiles, 1, own)
    for i, block in enumerate(blocks):
        pieces_ref[i] = block.astype(jnp.bfloat16)


def same_kernel(*refs):
    tiles, (left_ref, left_last_ref, pieces_ref) = refs[:3], refs[3:]
    blocks = lane_products(left_ref[...], left_last_ref[...], tiles, 0, pieces_ref.shape[2])
    for i, block in enumerate(blocks):
        pieces_ref[i] = block


def join_kernel(pieces_ref, other_ref, scale_ref, out_ref):
    blocks = [pieces_ref[i] + other_ref[i].astype(jnp.float32) for i in range(pieces_ref.shape[0])]
    space = out_ref.shape[1] - len(blocks) * blocks[0].shape[1]
    blocks.append(scale_tail(scale_ref[...], blocks[0].shape[0], space))
    out_ref[...] = side_by_side(blocks).astype(out_ref.dtype)


def lanes_image_kernel(own, *refs):
    parts_refs, out_ref = refs[:-1], refs[-1]
    half = len(parts_refs)
    count = parts_refs[0].shape[0]
    total, scales = [0.0] * half, [None] * half
    for m, ref in enumerate(parts_refs):
        part = ref[...].astype(jnp.float32)
        blocks = cut(part[:, : half * own], own)
        for j in range(half):
            total[j] = total[j] + blocks[j ^ m]
        scales[m] = scale_of(part[:, half * own :], own)
    gram, scaled = 0.0, []
    for j in range(half):
        image = total[j] * scales[j]
        gram = gram + lax.dot_general(
            image, image, NT, precision=HIGH, preferred_element_type=jnp.float32
        )
        scaled.append(image * scales[j])
    tail = gram_tail(gram)
    for j in range(half):
        high, low = two_parts(scaled[j])
        here = tail if j == 0 else jnp.zeros_like(tail)
        whole = with_tail(high.astype(jnp.float32), here, out_ref.shape[2])
        out_ref[j, 0:count, :] = whole.astype(jnp.bfloat16)
        whole = with_tail(low.astype(jnp.float32), jnp.zeros_like(tail), out_ref.shape[2])
        out_ref[j, count : 2 * count, :] = whole.astype(jnp.bfloat16)


def row_products(image_ref, tiles, odd, own):
    main_ref, side_ref, last_ref = tiles
    count = image_ref.shape[1] // 2
    lefts = [image_ref[i, :, 0:own] for i in range(image_ref.shape[0])]
    low, high, at = side_span(odd, own)
    padded = [lefts[-1]]
    for gap, place in ((at, 0), (high - low - at - own, len(padded) + 1)):
        if gap:
            padded.insert(place, jnp.zeros((2 * count, gap), jnp.bfloat16))
    main, whole = side_by_side(lefts[:-1]), side_by_side(lefts)
    values = []
    for pairs in (
        ((main, main_ref, 0, main.shape[1]), (side_by_side(padded), side_ref, low, high)),
        ((whole, last_ref, 0, whole.shape[1]),),
    ):
        total = pairs[0][1].shape[0]
        for i in range(0, total, 256):
            value = sum(
                lax.dot_general(
                    left, ref[i : min(i + 256, total), start:stop], NT,
                    preferred_element_type=jnp.float32,
                )
                for left, ref, start, stop in pairs
            )
            values.append(value[:count] + value[count:])
    return side_by_side(values)


def own_lanes_kernel(own, *refs):
    tiles, (image_ref, out_ref) = refs[:3], refs[3:]
    out_ref[...] = row_products(image_ref, tiles, 0, own)


def other_lanes_kernel(own, *refs):
    tiles, (own_image_ref, image_ref, line_ref), out_refs = refs[:3], refs[3:6], refs[6:]
    count = line_ref.shape[0]
    value = line_ref[...] + row_products(image_ref, tiles, 1, own)
    gram = 0.0
    for ref in (own_image_ref, image_ref):
        gram = gram + gram_of(ref[0, 0:count, :].astype(jnp.float32), own)
    tail = gram_tail(gram)
    for block, ref in zip(cut(value, own), out_refs):
        ref[...] = with_tail(block, tail, ref.shape[1]).astype(ref.dtype)


def eliminate(both, width, block=8):
    count, total = both.shape
    block = math.gcd(count, block)
    repeat = total // 128
    ids = lax.broadcasted_iota(jnp.int32, (count, 128), 0)
    roots = jnp.zeros((count, 128), jnp.float32)

    def wide(value):
        return side_by_side([value] * repeat)

    def down(value):
        return jnp.concatenate([value] * (count // 8), axis=0)

    for k in range(0, count, block):
        columns = [
            jnp.broadcast_to(both[:, width + k + t : width + k + t + 1], (count, 128))
            for t in range(block)
        ]
        corner = {
            (s, t): jnp.broadcast_to(columns[t][k + s : k + s + 1, :], (8, 128))
            for t in range(block)
            for s in range(t, block)
        }
        lines = [
            jnp.broadcast_to(both[k + t : k + t + 1, :], (8, total)) for t in range(block)
        ]
        for t in range(block):
            pivot = corner[t, t]
            inverse = 1.0 / pivot
            roots = jnp.where(ids == k + t, down(1.0 / jnp.sqrt(pivot)), roots)
            lower = {s: corner[s, t] * inverse for s in range(t + 1, block)}
            factor = columns[t] * down(inverse)
            for u in range(t + 1, block):
                columns[u] = columns[u] - factor * down(corner[u, t])
                lines[u] = lines[u] - wide(lower[u]) * lines[t]
                for s in range(u, block):
                    corner[s, u] = corner[s, u] - lower[s] * corner[u, t]
            factor = jnp.where(ids > k + t, factor, 0.0)
            both = both - wide(factor) * down(lines[t])
    return both * wide(roots)


def pack_square(square):
    count = square.shape[0]
    fold = max(1, min(count // 8, 128 // count))
    high = count // fold
    return jnp.concatenate([square[i * high : (i + 1) * high] for i in range(fold)], axis=1)


def unpack_square(packed, count):
    high = packed.shape[0]
    fold = count // high
    return jnp.concatenate(
        [packed[:, i * count : (i + 1) * count] for i in range(fold)], axis=0
    )


def image_kernel(*refs):
    pieces_refs, (scale_ref, image_ref, gram_ref, grams_ref) = refs[:-4], refs[-4:]
    width = scale_ref.shape[1]
    both = sum(ref[...].astype(jnp.float32) for ref in pieces_refs)
    gram_ref[...] = gram_of(both, width)
    image = both[:, :width] * scale_ref[...]
    image_ref[...] = image
    gram = lax.dot_general(image, image, NT, precision=HIGH, preferred_element_type=jnp.float32)
    packed = pack_square(gram)
    for i in range(grams_ref.shape[0]):
        grams_ref[i] = packed


def filled(parts):
    width = sum(p.shape[1] for p in parts)
    space = lanes(width) - width
    if space:
        parts = parts + [jnp.zeros((parts[0].shape[0], space), jnp.float32)]
    return side_by_side(parts)


def middle_kernel(image_ref, gram_ref, out_ref, inverse_ref):
    count, own = image_ref.shape
    rows = lax.broadcasted_iota(jnp.int32, (count, count), 0)
    unit = (rows == lax.broadcasted_iota(jnp.int32, (count, count), 1)).astype(jnp.float32)
    whole = eliminate(filled([image_ref[...], gram_ref[...], unit]), own)
    out_ref[...] = whole[:, :own]
    inverse_ref[...] = whole[:, own + count : own + 2 * count]


def last_kernel(image_ref, inverse_ref, grams_ref, out_ref):
    count, own = image_ref.shape
    inverse = inverse_ref[...]
    gram = unpack_square(jnp.sum(grams_ref[...], axis=0), count)
    gram = jnp.dot(inverse, gram, precision=HIGH, preferred_element_type=jnp.float32)
    gram = lax.dot_general(gram, inverse, NT, precision=HIGH, preferred_element_type=jnp.float32)
    out_ref[...] = eliminate(filled([image_ref[...], gram]), own)[:, :own]


NAMES = ("row_high", "row_low", "col_high", "col_mid", "core")
ROW_SET, LANE_SET = ("row_high", "col_mid"), ("row_low", "col_high", "core")


def swap(value, axes, offset):
    size = lax.axis_size(axes)
    return lax.ppermute(value, axes, [(i, i ^ offset) for i in range(size)])


def local(embeddings, start_vectors):
    rows, cols = lax.axis_size(ROW_SET), lax.axis_size(LANE_SET)
    own, width = embeddings.shape
    count = start_vectors.shape[0]
    f32, bf16 = jnp.float32, jnp.bfloat16
    half = cols // 2
    even = [*range(0, cols, 2)]
    padded = lanes(own + 1)

    unit, starts = call(own_kernel, [((own, width), bf16), ((count, own), bf16)])(
        embeddings, start_vectors
    )
    row_blocks, lane_blocks = {0: embeddings}, {0: embeddings}
    tops = [m for m in range(1, rows) if m.bit_count() == 1]
    bits = [1 << i for i in range(cols.bit_length() - 2, -1, -1)]
    for m in bits:
        lane_blocks[m] = swap(embeddings, LANE_SET, m)
    unit, lane_blocks[bits[0]] = lax.optimization_barrier((unit, lane_blocks[bits[0]]))
    for m in even:
        if m.bit_count() > 1:
            lane_blocks[m] = swap(lane_blocks[m & (m - 1)], LANE_SET, m & -m)
    first = [(lane_blocks, m, lane_blocks[m]) for m in bits[:0:-1]]
    first += [(row_blocks, m, swap(embeddings, ROW_SET, m)) for m in tops]
    blocks, unit, starts = lax.optimization_barrier(([f[2] for f in first], unit, starts))
    for (where, m, _), block in zip(first, blocks):
        where[m] = block
    for m in even[1:-1]:
        lane_blocks[m + 1] = swap(lane_blocks[m], LANE_SET, 1)
    for m in range(rows):
        if m.bit_count() > 1:
            row_blocks[m] = swap(row_blocks[m & (m - 1)], ROW_SET, m & -m)

    high, deep = (rows - 1) * own, (half - 1) * own
    unit, farthest = lax.optimization_barrier((unit, lane_blocks[even[-1]]))
    main_rows, even_lanes, odd_lanes, even_main, odd_main, fold = call(
        functools.partial(main_kernel, rows - 1),
        [
            ((high, width), bf16),
            ((deep, width), bf16),
            ((deep, width), bf16),
            ((high, deep), bf16),
            ((high, deep), bf16),
            ((high, 128), f32),
        ],
        flops=4 * high * deep * width,
    )(
        unit,
        *[row_blocks[m] for m in range(1, rows - 1)],
        *[lane_blocks[m] for m in even[1:-1]],
        *[lane_blocks[m + 1] for m in even[:-1]],
    )
    lines = count + -(-2 * rows // 8) * 8
    side, even_last, odd_last, sums, send = call(
        rest_kernel,
        [
            ((high, 2 * own), bf16),
            ((own, half * own), bf16),
            ((own, half * own), bf16),
            ((rows, own), f32),
            ((lines, own), bf16),
        ],
        [
            pltpu.VMEM((own, width), bf16),
            pltpu.VMEM((half * own, width), bf16),
            pltpu.VMEM((half * own, width), bf16),
            pltpu.VMEM((2 * own, width), bf16),
            pltpu.VMEM((high, 128), f32),
            pltpu.VMEM((own, 128), f32),
        ],
        flops=4 * (high + half * own) * own * width,
    )(
        main_rows,
        fold,
        even_lanes,
        odd_lanes,
        row_blocks[rows - 1],
        farthest,
        swap(farthest, LANE_SET, 1),
        starts,
    )
    even_tiles = (even_main, side, even_last)
    odd_tiles = (odd_main, side, odd_last)

    came = [swap(send, ROW_SET, m) for m in range(1, rows)]
    other, left, left_last, degrees, scale = call(
        first_kernel,
        [
            ((half, count, own), bf16),
            ((count, high), bf16),
            ((count, own), bf16),
            ((1, own), f32),
            ((1, own), f32),
        ],
    )(*odd_tiles, sums, starts, *came)
    other = swap(other, LANE_SET, 1)
    (pieces,) = call(
        same_kernel,
        [((half, count, own), f32)],
        flops=2 * count * rows * half * own * own,
    )(*even_tiles, left, left_last)
    (parts,) = call(join_kernel, [((count, lanes(half * own + 128)), bf16)])(pieces, other, scale)
    parts = [parts] + [swap(parts, LANE_SET, m) for m in even[1:]]

    (image,) = call(functools.partial(lanes_image_kernel, own), [((half, 2 * count, padded), bf16)])(*parts)
    other = swap(image, LANE_SET, 1)
    (value,) = call(
        functools.partial(own_lanes_kernel, own),
        [((count, rows * own), f32)],
        flops=4 * count * rows * half * own * own,
    )(*even_tiles, image)
    wide = lanes(own + 2 * count)
    pieces = call(
        functools.partial(other_lanes_kernel, own),
        [((count, wide), f32 if m == 0 else bf16) for m in range(rows)],
    )(*odd_tiles, image, other, value)
    moved = [swap(pieces[m], ROW_SET, m) for m in range(rows - 1, 0, -1)]
    fold = max(1, min(count // 8, 128 // count))
    image, gram, grams = call(
        image_kernel,
        [
            ((count, own), f32),
            ((count, count), f32),
            ((rows * cols, count // fold, count * fold), f32),
        ],
    )(pieces[0], *moved, scale)
    grams = lax.all_to_all(grams, NAMES, 0, 0, tiled=True)
    image, inverse = call(middle_kernel, [((count, own), f32), ((count, count), f32)])(image, gram)
    (vectors,) = call(last_kernel, [((count, own), f32)])(image, inverse, grams)
    return (vectors, degrees.reshape(own))


def solution(mesh):
    row_size, col_size = mesh.shape["row"], mesh.shape["col"]
    devices = mesh.devices.reshape(row_size // 2, 2, 2, col_size // 4, 2)
    return jax.shard_map(
        local,
        mesh=jax.sharding.Mesh(devices, NAMES),
        in_specs=(P(NAMES, None), P(None, NAMES)),
        out_specs=(P(None, NAMES), P(NAMES)),
        check_vma=False,
    )
```

```python
import functools
import math

import jax
import jax.numpy as jnp
from jax import lax
from jax.experimental import pallas as pl
from jax.experimental.pallas import tpu as pltpu
from jax.sharding import PartitionSpec as P

VMEM = pl.BlockSpec(memory_space=pltpu.VMEM)
NT = (((1,), (1,)), ((), ()))
HIGH = lax.Precision.HIGHEST


def lanes(width):
    return -(-width // 128) * 128


def call(kernel, out_shapes, scratch=(), flops=0):
    count = len(out_shapes)
    mib = 1024 * 1024

    def run(*operands):
        needs = sum(math.prod(o.shape) * jnp.dtype(o.dtype).itemsize for o in operands)
        needs += sum(math.prod(s) * jnp.dtype(d).itemsize for s, d in out_shapes)
        limit = min(56 * mib, 2 * needs // mib * mib + 8 * mib)
        return pl.pallas_call(
            kernel,
            out_shape=[jax.ShapeDtypeStruct(s, d) for s, d in out_shapes],
            in_specs=[VMEM] * len(operands),
            out_specs=[VMEM] * count,
            scratch_shapes=list(scratch),
            compiler_params=pltpu.CompilerParams(vmem_limit_bytes=limit),
            cost_estimate=pl.CostEstimate(flops=flops, bytes_accessed=0, transcendentals=0),
        )(*operands)

    return run


def side_by_side(blocks):
    return jnp.concatenate(blocks, axis=1) if len(blocks) > 1 else blocks[0]


def cut(value, width):
    return [value[:, i : i + width] for i in range(0, value.shape[1], width)]


def two_parts(value):
    high = value.astype(jnp.bfloat16)
    return high, (value - high.astype(jnp.float32)).astype(jnp.bfloat16)


def unit_rows(ref, gain):
    values = ref[...].astype(jnp.float32)
    power = jnp.mean(values * values, axis=1, keepdims=True)
    factor = lax.rsqrt(power + 1e-06) * (gain / math.sqrt(ref.shape[1]))
    return (values * factor).astype(jnp.bfloat16)


def own_kernel(emb_ref, start_ref, unit_ref, out_ref):
    unit_ref[...] = unit_rows(emb_ref, 1.0)
    out_ref[...] = start_ref[...].astype(out_ref.dtype)


def affinity(rows_ref, parts, own, fold_ref, more_ref=None):
    def row_block(start):
        piece = rows_ref[pl.ds(start, own), :]
        fold = 0.0 if more_ref is None else more_ref[pl.ds(start, own), :]
        for lanes_ref, first, tile_ref in parts:
            total = tile_ref.shape[1]
            for j in range(0, total, 256):
                stop = min(j + 256, total)
                inner = lax.dot_general(
                    piece, lanes_ref[first + j : first + stop, :], NT,
                    preferred_element_type=jnp.float32,
                )
                values = jnp.exp(inner - 8.0)
                tile_ref[pl.ds(start, own), j:stop] = values.astype(jnp.bfloat16)
                for part in cut(values, 128):
                    gap = 128 - part.shape[1]
                    if gap:
                        part = side_by_side([part, jnp.zeros((own, gap), jnp.float32)])
                    fold = fold + part
        fold_ref[pl.ds(start, own), :] = fold

    count = rows_ref.shape[0] // own
    if count <= 4:
        for i in range(count):
            row_block(i * own)
    else:
        pl.loop(0, count)(lambda i: row_block(pl.multiple_of(i * own, own)))


def unfold(fold):
    ones = jnp.ones((8, fold.shape[1]), jnp.float32)
    sums = lax.dot_general(ones, fold, NT, precision=HIGH, preferred_element_type=jnp.float32)
    return sums[0:1, :]


def main_kernel(rows, unit_ref, *refs):
    row_refs, lane_refs = refs[: rows - 1], refs[rows - 1 : -6]
    rows_ref, even_ref, odd_ref, even_tile_ref, odd_tile_ref, fold_ref = refs[-6:]
    own = unit_ref.shape[0]
    rows_ref[0:own, :] = unit_ref[...] * 8
    even_ref[0:own, :] = unit_ref[...]
    for i, ref in enumerate(row_refs, 1):
        rows_ref[i * own : (i + 1) * own, :] = unit_rows(ref, 8.0)
    half = even_ref.shape[0] // own
    for i, ref in enumerate(lane_refs, 1):
        target, at = (even_ref, i) if i < half else (odd_ref, i - half)
        target[at * own : (at + 1) * own, :] = unit_rows(ref, 1.0)
    parts = [(even_ref, 0, even_tile_ref), (odd_ref, 0, odd_tile_ref)]
    affinity(rows_ref, parts, own, fold_ref)


def rest_kernel(rows_ref, fold_in_ref, even_ref, odd_in_ref, *refs):
    row_ref, fresh_ref, start_ref = refs[:3]
    side_tile_ref, even_last_ref, odd_last_ref, sums_ref, send_ref = refs[3:8]
    last_ref, odd_ref, fold_ref, fold_last_ref = refs[8:]
    own = row_ref.shape[0]
    high = odd_in_ref.shape[0]
    odd_ref[0:high, :] = odd_in_ref[...]
    odd_ref[high : high + own, :] = unit_rows(fresh_ref, 1.0)
    affinity(rows_ref, [(odd_ref, high, side_tile_ref)], own, fold_ref, fold_in_ref)
    last_ref[...] = unit_rows(row_ref, 8.0)
    parts = [(even_ref, 0, even_last_ref), (odd_ref, 0, odd_last_ref)]
    affinity(last_ref, parts, own, fold_last_ref)
    lines = cut(unfold(fold_ref[...]), own) + [unfold(fold_last_ref[...])]
    sums = jnp.concatenate(lines, axis=0)
    sums_ref[...] = sums
    parts = [start_ref[...].astype(jnp.float32)]
    parts += [part.astype(jnp.float32) for part in two_parts(sums)]
    space = send_ref.shape[0] - sum(p.shape[0] for p in parts)
    if space:
        parts.append(jnp.zeros((space, own), jnp.float32))
    send_ref[...] = jnp.concatenate(parts, axis=0).astype(jnp.bfloat16)


def lane_products(left, last, tiles, own):
    def product(value, ref):
        return side_by_side(
            [
                jnp.dot(value, ref[:, i : i + 256], preferred_element_type=jnp.float32)
                for i in range(0, ref.shape[1], 256)
            ]
        )

    blocks = [block for ref in tiles[:-1] for block in cut(product(left, ref), own)]
    return [x + y for x, y in zip(blocks, cut(product(last, tiles[-1]), own))]


def with_tail(block, tail, width):
    space = width - block.shape[1] - tail.shape[1]
    parts = [block, tail]
    if space:
        parts.append(jnp.zeros((block.shape[0], space), jnp.float32))
    return side_by_side(parts)


def gram_tail(gram):
    return side_by_side([p.astype(jnp.float32) for p in two_parts(gram)])


def gram_of(piece, own):
    count = piece.shape[0]
    return piece[:, own : own + count] + piece[:, own + count : own + 2 * count]


def scale_tail(scale, count, space):
    lines = []
    for part in two_parts(scale):
        for piece in cut(part.astype(jnp.float32), space):
            gap = space - piece.shape[1]
            lines.append(side_by_side([piece, jnp.zeros((1, gap), jnp.float32)]) if gap else piece)
    lines.append(jnp.zeros((count - len(lines), space), jnp.float32))
    return jnp.concatenate(lines, axis=0)


def scale_of(tail, own):
    lines = -(-own // tail.shape[1])
    parts = [
        side_by_side([tail[k + i : k + i + 1] for i in range(lines)])[:, :own]
        for k in (0, lines)
    ]
    return parts[0] + parts[1]


def first_kernel(*refs):
    tiles, refs = refs[:3], refs[3:]
    sums_ref, start_ref, came_refs = refs[0], refs[1], refs[2:-5]
    pieces_ref, left_ref, left_last_ref, degrees_ref, scale_ref = refs[-5:]
    count, own = start_ref.shape
    rows = sums_ref.shape[0]
    sums, starts = [sums_ref[...]], [start_ref[...].astype(jnp.float32)]
    for ref in came_refs:
        came = ref[...].astype(jnp.float32)
        starts.append(came[:count])
        high, low = (came[count + i * rows : count + (i + 1) * rows] for i in range(2))
        sums.append(high + low)
    degrees = []
    for j in range(rows):
        degrees.append(sum(s[j ^ m : (j ^ m) + 1, :] for m, s in enumerate(sums)))
    degrees_ref[...] = degrees[0]
    scales = [1.0 / jnp.sqrt(d) for d in degrees]
    scale_ref[...] = scales[0]
    scaled = [(start * scale).astype(jnp.bfloat16) for start, scale in zip(starts, scales)]
    left_ref[...] = side_by_side(scaled[:-1])
    left_last_ref[...] = scaled[-1]
    blocks = lane_products(left_ref[...], left_last_ref[...], tiles, own)
    for i, block in enumerate(blocks):
        pieces_ref[i] = block.astype(jnp.bfloat16)


def same_kernel(*refs):
    tiles, (left_ref, left_last_ref, pieces_ref) = refs[:2], refs[2:]
    blocks = lane_products(left_ref[...], left_last_ref[...], tiles, pieces_ref.shape[2])
    for i, block in enumerate(blocks):
        pieces_ref[i] = block


def join_kernel(pieces_ref, other_ref, scale_ref, out_ref):
    blocks = [pieces_ref[i] + other_ref[i].astype(jnp.float32) for i in range(pieces_ref.shape[0])]
    space = out_ref.shape[1] - len(blocks) * blocks[0].shape[1]
    blocks.append(scale_tail(scale_ref[...], blocks[0].shape[0], space))
    out_ref[...] = side_by_side(blocks).astype(out_ref.dtype)


def lanes_image_kernel(own, *refs):
    parts_refs, out_ref = refs[:-1], refs[-1]
    half = len(parts_refs)
    count = parts_refs[0].shape[0]
    total, scales = [0.0] * half, [None] * half
    for m, ref in enumerate(parts_refs):
        part = ref[...].astype(jnp.float32)
        blocks = cut(part[:, : half * own], own)
        for j in range(half):
            total[j] = total[j] + blocks[j ^ m]
        scales[m] = scale_of(part[:, half * own :], own)
    gram, scaled = 0.0, []
    for j in range(half):
        image = total[j] * scales[j]
        gram = gram + lax.dot_general(
            image, image, NT, precision=HIGH, preferred_element_type=jnp.float32
        )
        scaled.append(image * scales[j])
    tail = gram_tail(gram)
    for j in range(half):
        high, low = two_parts(scaled[j])
        here = tail if j == 0 else jnp.zeros_like(tail)
        whole = with_tail(high.astype(jnp.float32), here, out_ref.shape[2])
        out_ref[j, 0:count, :] = whole.astype(jnp.bfloat16)
        whole = with_tail(low.astype(jnp.float32), jnp.zeros_like(tail), out_ref.shape[2])
        out_ref[j, count : 2 * count, :] = whole.astype(jnp.bfloat16)


def row_products(image_ref, tiles, own):
    count = image_ref.shape[1] // 2
    whole = side_by_side([image_ref[i, :, 0:own] for i in range(image_ref.shape[0])])
    values = []
    for refs in (tiles[:-1], tiles[-1:]):
        total = refs[0].shape[0]
        for i in range(0, total, 256):
            value, at = 0.0, 0
            for ref in refs:
                value = value + lax.dot_general(
                    whole[:, at : at + ref.shape[1]], ref[i : min(i + 256, total), :], NT,
                    preferred_element_type=jnp.float32,
                )
                at += ref.shape[1]
            values.append(value[:count] + value[count:])
    return side_by_side(values)


def own_lanes_kernel(own, *refs):
    tiles, (image_ref, out_ref) = refs[:2], refs[2:]
    out_ref[...] = row_products(image_ref, tiles, own)


def other_lanes_kernel(own, *refs):
    tiles, (own_image_ref, image_ref, line_ref), out_refs = refs[:3], refs[3:6], refs[6:]
    count = line_ref.shape[0]
    value = line_ref[...] + row_products(image_ref, tiles, own)
    gram = 0.0
    for ref in (own_image_ref, image_ref):
        gram = gram + gram_of(ref[0, 0:count, :].astype(jnp.float32), own)
    tail = gram_tail(gram)
    for block, ref in zip(cut(value, own), out_refs):
        ref[...] = with_tail(block, tail, ref.shape[1]).astype(ref.dtype)


def eliminate(both, width, block=8):
    count, total = both.shape
    block = math.gcd(count, block)
    repeat = total // 128
    ids = lax.broadcasted_iota(jnp.int32, (count, 128), 0)
    roots = jnp.zeros((count, 128), jnp.float32)

    def wide(value):
        return side_by_side([value] * repeat)

    def down(value):
        return jnp.concatenate([value] * (count // 8), axis=0)

    for k in range(0, count, block):
        columns = [
            jnp.broadcast_to(both[:, width + k + t : width + k + t + 1], (count, 128))
            for t in range(block)
        ]
        corner = {
            (s, t): jnp.broadcast_to(columns[t][k + s : k + s + 1, :], (8, 128))
            for t in range(block)
            for s in range(t, block)
        }
        lines = [
            jnp.broadcast_to(both[k + t : k + t + 1, :], (8, total)) for t in range(block)
        ]
        for t in range(block):
            pivot = corner[t, t]
            inverse = 1.0 / pivot
            roots = jnp.where(ids == k + t, down(1.0 / jnp.sqrt(pivot)), roots)
            lower = {s: corner[s, t] * inverse for s in range(t + 1, block)}
            factor = columns[t] * down(inverse)
            for u in range(t + 1, block):
                columns[u] = columns[u] - factor * down(corner[u, t])
                lines[u] = lines[u] - wide(lower[u]) * lines[t]
                for s in range(u, block):
                    corner[s, u] = corner[s, u] - lower[s] * corner[u, t]
            factor = jnp.where(ids > k + t, factor, 0.0)
            both = both - wide(factor) * down(lines[t])
    return both * wide(roots)


def pack_square(square):
    count = square.shape[0]
    fold = max(1, min(count // 8, 128 // count))
    high = count // fold
    return jnp.concatenate([square[i * high : (i + 1) * high] for i in range(fold)], axis=1)


def unpack_square(packed, count):
    high = packed.shape[0]
    fold = count // high
    return jnp.concatenate(
        [packed[:, i * count : (i + 1) * count] for i in range(fold)], axis=0
    )


def image_kernel(*refs):
    pieces_refs, (scale_ref, image_ref, gram_ref, grams_ref) = refs[:-4], refs[-4:]
    width = scale_ref.shape[1]
    both = sum(ref[...].astype(jnp.float32) for ref in pieces_refs)
    gram_ref[...] = gram_of(both, width)
    image = both[:, :width] * scale_ref[...]
    image_ref[...] = image
    gram = lax.dot_general(image, image, NT, precision=HIGH, preferred_element_type=jnp.float32)
    packed = pack_square(gram)
    for i in range(grams_ref.shape[0]):
        grams_ref[i] = packed


def filled(parts):
    width = sum(p.shape[1] for p in parts)
    space = lanes(width) - width
    if space:
        parts = parts + [jnp.zeros((parts[0].shape[0], space), jnp.float32)]
    return side_by_side(parts)


def middle_kernel(image_ref, gram_ref, out_ref, inverse_ref):
    count, own = image_ref.shape
    rows = lax.broadcasted_iota(jnp.int32, (count, count), 0)
    unit = (rows == lax.broadcasted_iota(jnp.int32, (count, count), 1)).astype(jnp.float32)
    whole = eliminate(filled([image_ref[...], gram_ref[...], unit]), own)
    out_ref[...] = whole[:, :own]
    inverse_ref[...] = whole[:, own + count : own + 2 * count]


def last_kernel(image_ref, inverse_ref, grams_ref, out_ref):
    count, own = image_ref.shape
    inverse = inverse_ref[...]
    gram = unpack_square(jnp.sum(grams_ref[...], axis=0), count)
    gram = jnp.dot(inverse, gram, precision=HIGH, preferred_element_type=jnp.float32)
    gram = lax.dot_general(gram, inverse, NT, precision=HIGH, preferred_element_type=jnp.float32)
    out_ref[...] = eliminate(filled([image_ref[...], gram]), own)[:, :own]


NAMES = ("row_high", "row_low", "col_high", "col_mid", "core")
ROW_SET, LANE_SET = ("row_high", "col_mid"), ("row_low", "col_high", "core")


def swap(value, axes, offset):
    size = lax.axis_size(axes)
    return lax.ppermute(value, axes, [(i, i ^ offset) for i in range(size)])


def local(embeddings, start_vectors):
    rows, cols = lax.axis_size(ROW_SET), lax.axis_size(LANE_SET)
    own, width = embeddings.shape
    count = start_vectors.shape[0]
    f32, bf16 = jnp.float32, jnp.bfloat16
    half = cols // 2
    even = [*range(0, cols, 2)]
    padded = lanes(own + 1)

    unit, starts = call(own_kernel, [((own, width), bf16), ((count, own), bf16)])(
        embeddings, start_vectors
    )
    row_blocks, lane_blocks = {0: embeddings}, {0: embeddings}
    tops = [m for m in range(1, rows) if m.bit_count() == 1]
    bits = [1 << i for i in range(cols.bit_length() - 2, -1, -1)]
    for m in bits:
        lane_blocks[m] = swap(embeddings, LANE_SET, m)
    unit, lane_blocks[bits[0]] = lax.optimization_barrier((unit, lane_blocks[bits[0]]))
    for m in even:
        if m.bit_count() > 1:
            lane_blocks[m] = swap(lane_blocks[m & (m - 1)], LANE_SET, m & -m)
    first = [(lane_blocks, m, lane_blocks[m]) for m in bits[:0:-1]]
    first += [(row_blocks, m, swap(embeddings, ROW_SET, m)) for m in tops]
    blocks, unit, starts = lax.optimization_barrier(([f[2] for f in first], unit, starts))
    for (where, m, _), block in zip(first, blocks):
        where[m] = block
    for m in even[1:-1]:
        lane_blocks[m + 1] = swap(lane_blocks[m], LANE_SET, 1)
    for m in range(rows):
        if m.bit_count() > 1:
            row_blocks[m] = swap(row_blocks[m & (m - 1)], ROW_SET, m & -m)

    high, deep = (rows - 1) * own, (half - 1) * own
    unit, farthest = lax.optimization_barrier((unit, lane_blocks[even[-1]]))
    lane_blocks[even[-1]] = farthest
    main_rows, even_lanes, odd_lanes, even_main, odd_main, fold = call(
        functools.partial(main_kernel, rows - 1),
        [
            ((high, width), bf16),
            ((half * own, width), bf16),
            ((deep, width), bf16),
            ((high, half * own), bf16),
            ((high, deep), bf16),
            ((high, 128), f32),
        ],
        flops=2 * high * (half * own + deep) * width,
    )(
        unit,
        *[row_blocks[m] for m in range(1, rows - 1)],
        *[lane_blocks[m] for m in even[1:]],
        *[lane_blocks[m + 1] for m in even[:-1]],
    )
    lines = count + -(-2 * rows // 8) * 8
    odd_side, even_last, odd_last, sums, send = call(
        rest_kernel,
        [
            ((high, own), bf16),
            ((own, half * own), bf16),
            ((own, half * own), bf16),
            ((rows, own), f32),
            ((lines, own), bf16),
        ],
        [
            pltpu.VMEM((own, width), bf16),
            pltpu.VMEM((half * own, width), bf16),
            pltpu.VMEM((high, 128), f32),
            pltpu.VMEM((own, 128), f32),
        ],
        flops=2 * (high + cols * own) * own * width,
    )(
        main_rows,
        fold,
        even_lanes,
        odd_lanes,
        row_blocks[rows - 1],
        swap(farthest, LANE_SET, 1),
        starts,
    )
    even_tiles = (even_main, even_last)
    odd_tiles = (odd_main, odd_side, odd_last)

    came = [swap(send, ROW_SET, m) for m in range(1, rows)]
    other, left, left_last, degrees, scale = call(
        first_kernel,
        [
            ((half, count, own), bf16),
            ((count, high), bf16),
            ((count, own), bf16),
            ((1, own), f32),
            ((1, own), f32),
        ],
    )(*odd_tiles, sums, starts, *came)
    other = swap(other, LANE_SET, 1)
    (pieces,) = call(
        same_kernel,
        [((half, count, own), f32)],
        flops=2 * count * rows * half * own * own,
    )(*even_tiles, left, left_last)
    (parts,) = call(join_kernel, [((count, lanes(half * own + 128)), bf16)])(pieces, other, scale)
    parts = [parts] + [swap(parts, LANE_SET, m) for m in even[1:]]

    (image,) = call(functools.partial(lanes_image_kernel, own), [((half, 2 * count, padded), bf16)])(*parts)
    other = swap(image, LANE_SET, 1)
    (value,) = call(
        functools.partial(own_lanes_kernel, own),
        [((count, rows * own), f32)],
        flops=4 * count * rows * half * own * own,
    )(*even_tiles, image)
    wide = lanes(own + 2 * count)
    pieces = call(
        functools.partial(other_lanes_kernel, own),
        [((count, wide), f32 if m == 0 else bf16) for m in range(rows)],
    )(*odd_tiles, image, other, value)
    moved = [swap(pieces[m], ROW_SET, m) for m in range(rows - 1, 0, -1)]
    fold = max(1, min(count // 8, 128 // count))
    image, gram, grams = call(
        image_kernel,
        [
            ((count, own), f32),
            ((count, count), f32),
            ((rows * cols, count // fold, count * fold), f32),
        ],
    )(pieces[0], *moved, scale)
    grams = lax.all_to_all(grams, NAMES, 0, 0, tiled=True)
    image, inverse = call(middle_kernel, [((count, own), f32), ((count, count), f32)])(image, gram)
    (vectors,) = call(last_kernel, [((count, own), f32)])(image, inverse, grams)
    return (vectors, degrees.reshape(own))


def solution(mesh):
    row_size, col_size = mesh.shape["row"], mesh.shape["col"]
    devices = mesh.devices.reshape(row_size // 2, 2, 2, col_size // 4, 2)
    return jax.shard_map(
        local,
        mesh=jax.sharding.Mesh(devices, NAMES),
        in_specs=(P(NAMES, None), P(None, NAMES)),
        out_specs=(P(None, NAMES), P(NAMES)),
        check_vma=False,
    )
```

```python
import functools
import math

import jax
import jax.numpy as jnp
from jax import lax
from jax.experimental import pallas as pl
from jax.experimental.pallas import tpu as pltpu
from jax.sharding import PartitionSpec as P

VMEM = pl.BlockSpec(memory_space=pltpu.VMEM)
NT = (((1,), (1,)), ((), ()))
HIGH = lax.Precision.HIGHEST


def lanes(width):
    return -(-width // 128) * 128


def call(kernel, out_shapes, scratch=(), flops=0):
    count = len(out_shapes)
    mib = 1024 * 1024

    def run(*operands):
        needs = sum(math.prod(o.shape) * jnp.dtype(o.dtype).itemsize for o in operands)
        needs += sum(math.prod(s) * jnp.dtype(d).itemsize for s, d in out_shapes)
        limit = min(56 * mib, 2 * needs // mib * mib + 8 * mib)
        return pl.pallas_call(
            kernel,
            out_shape=[jax.ShapeDtypeStruct(s, d) for s, d in out_shapes],
            in_specs=[VMEM] * len(operands),
            out_specs=[VMEM] * count,
            scratch_shapes=list(scratch),
            compiler_params=pltpu.CompilerParams(vmem_limit_bytes=limit),
            cost_estimate=pl.CostEstimate(flops=flops, bytes_accessed=0, transcendentals=0),
        )(*operands)

    return run


def side_by_side(blocks):
    return jnp.concatenate(blocks, axis=1) if len(blocks) > 1 else blocks[0]


def cut(value, width):
    return [value[:, i : i + width] for i in range(0, value.shape[1], width)]


def two_parts(value):
    high = value.astype(jnp.bfloat16)
    return high, (value - high.astype(jnp.float32)).astype(jnp.bfloat16)


def unit_rows(ref, gain):
    values = ref[...].astype(jnp.float32)
    power = jnp.mean(values * values, axis=1, keepdims=True)
    factor = lax.rsqrt(power + 1e-06) * (gain / math.sqrt(ref.shape[1]))
    return (values * factor).astype(jnp.bfloat16)


def own_kernel(emb_ref, start_ref, unit_ref, out_ref):
    unit_ref[...] = unit_rows(emb_ref, 1.0)
    out_ref[...] = start_ref[...].astype(out_ref.dtype)


def stack_kernel(first_ref, second_ref, out_ref):
    half = first_ref.shape[0]
    out_ref[0:half, :] = first_ref[...]
    out_ref[half : 2 * half, :] = second_ref[...]


def affinity(rows_ref, parts, own, fold_ref, more_ref=None):
    def row_block(start):
        piece = rows_ref[pl.ds(start, own), :]
        fold = 0.0 if more_ref is None else more_ref[pl.ds(start, own), :]
        for lanes_ref, first, tile_ref in parts:
            total = tile_ref.shape[1]
            for j in range(0, total, 256):
                stop = min(j + 256, total)
                inner = lax.dot_general(
                    piece, lanes_ref[first + j : first + stop, :], NT,
                    preferred_element_type=jnp.float32,
                )
                values = jnp.exp(inner - 8.0)
                tile_ref[pl.ds(start, own), j:stop] = values.astype(jnp.bfloat16)
                for part in cut(values, 128):
                    gap = 128 - part.shape[1]
                    if gap:
                        part = side_by_side([part, jnp.zeros((own, gap), jnp.float32)])
                    fold = fold + part
        fold_ref[pl.ds(start, own), :] = fold

    count = rows_ref.shape[0] // own
    if count <= 4:
        for i in range(count):
            row_block(i * own)
    else:
        pl.loop(0, count)(lambda i: row_block(pl.multiple_of(i * own, own)))


def unfold(fold):
    ones = jnp.ones((8, fold.shape[1]), jnp.float32)
    sums = lax.dot_general(ones, fold, NT, precision=HIGH, preferred_element_type=jnp.float32)
    return sums[0:1, :]


def main_kernel(rows, unit_ref, *refs):
    row_refs, lane_refs = refs[: rows - 1], refs[rows - 1 : -6]
    rows_ref, even_ref, odd_ref, even_tile_ref, odd_tile_ref, fold_ref = refs[-6:]
    own = unit_ref.shape[0]
    rows_ref[0:own, :] = unit_ref[...] * 8
    even_ref[0:own, :] = unit_ref[...]
    for i, ref in enumerate(row_refs, 1):
        rows_ref[i * own : (i + 1) * own, :] = unit_rows(ref, 8.0)
    half = even_ref.shape[0] // own
    for i, ref in enumerate(lane_refs, 1):
        target, at = (even_ref, i) if i < half else (odd_ref, i - half)
        target[at * own : (at + 1) * own, :] = unit_rows(ref, 1.0)
    parts = [(even_ref, 0, even_tile_ref), (odd_ref, 0, odd_tile_ref)]
    affinity(rows_ref, parts, own, fold_ref)


def rest_kernel(rows_ref, fold_in_ref, even_ref, odd_in_ref, row_ref, fresh_ref, *refs):
    start_refs, refs = refs[:-9], refs[-9:]
    side_tile_ref, even_last_ref, odd_last_ref, sums_ref, send_ref = refs[:5]
    last_ref, odd_ref, fold_ref, fold_last_ref = refs[5:]
    own = row_ref.shape[0]
    high = odd_in_ref.shape[0]
    odd_ref[0:high, :] = odd_in_ref[...]
    odd_ref[high : high + own, :] = unit_rows(fresh_ref, 1.0)
    affinity(rows_ref, [(odd_ref, high, side_tile_ref)], own, fold_ref, fold_in_ref)
    last_ref[...] = unit_rows(row_ref, 8.0)
    parts = [(even_ref, 0, even_last_ref), (odd_ref, 0, odd_last_ref)]
    affinity(last_ref, parts, own, fold_last_ref)
    lines = cut(unfold(fold_ref[...]), own) + [unfold(fold_last_ref[...])]
    sums = jnp.concatenate(lines, axis=0)
    sums_ref[...] = sums
    parts = [ref[...].astype(jnp.float32) for ref in start_refs]
    parts += [part.astype(jnp.float32) for part in two_parts(sums)]
    space = send_ref.shape[0] - sum(p.shape[0] for p in parts)
    if space:
        parts.append(jnp.zeros((space, own), jnp.float32))
    send_ref[...] = jnp.concatenate(parts, axis=0).astype(jnp.bfloat16)


def lane_products(left, last, tiles, own):
    def product(value, ref):
        return side_by_side(
            [
                jnp.dot(value, ref[:, i : i + 256], preferred_element_type=jnp.float32)
                for i in range(0, ref.shape[1], 256)
            ]
        )

    blocks = [block for ref in tiles[:-1] for block in cut(product(left, ref), own)]
    return [x + y for x, y in zip(blocks, cut(product(last, tiles[-1]), own))]


def with_tail(block, tail, width):
    space = width - block.shape[1] - tail.shape[1]
    parts = [block, tail]
    if space:
        parts.append(jnp.zeros((block.shape[0], space), jnp.float32))
    return side_by_side(parts)


def gram_tail(gram):
    return side_by_side([p.astype(jnp.float32) for p in two_parts(gram)])


def gram_of(piece, own):
    count = piece.shape[0]
    return piece[:, own : own + count] + piece[:, own + count : own + 2 * count]


def scale_tail(scale, count, space):
    lines = []
    for part in two_parts(scale):
        for piece in cut(part.astype(jnp.float32), space):
            gap = space - piece.shape[1]
            lines.append(side_by_side([piece, jnp.zeros((1, gap), jnp.float32)]) if gap else piece)
    lines.append(jnp.zeros((count - len(lines), space), jnp.float32))
    return jnp.concatenate(lines, axis=0)


def scale_of(tail, own):
    lines = -(-own // tail.shape[1])
    parts = [
        side_by_side([tail[k + i : k + i + 1] for i in range(lines)])[:, :own]
        for k in (0, lines)
    ]
    return parts[0] + parts[1]


def first_kernel(held, steps, *refs):
    tiles, start_refs = refs[:3], refs[3 : 3 + steps]
    near_ref, sums_refs = refs[3 + steps], refs[4 + steps : -5]
    pieces_ref, left_ref, left_last_ref, degrees_ref, scale_ref = refs[-5:]
    rows, own = sums_refs[0].shape
    count = pieces_ref.shape[1]
    near = near_ref[...].astype(jnp.float32)
    here = len(held) * count
    sums = [ref[...] for ref in sums_refs]
    sums.insert(1, near[here : here + rows] + near[here + rows : here + 2 * rows])
    blocks = [ref[...].astype(jnp.float32) for ref in start_refs] + [near[:here]]
    blocks = [b[i : i + count] for b in blocks for i in range(0, b.shape[0], count)]
    places = held + [m ^ 1 for m in held]
    starts = [blocks[places.index(j)] for j in range(rows)]
    degrees = []
    for j in range(rows):
        degrees.append(sum(s[j ^ m : (j ^ m) + 1, :] for m, s in enumerate(sums)))
    degrees_ref[...] = degrees[0]
    scales = [1.0 / jnp.sqrt(d) for d in degrees]
    scale_ref[...] = scales[0]
    scaled = [(start * scale).astype(jnp.bfloat16) for start, scale in zip(starts, scales)]
    left_ref[...] = side_by_side(scaled[:-1])
    left_last_ref[...] = scaled[-1]
    blocks = lane_products(left_ref[...], left_last_ref[...], tiles, own)
    for i, block in enumerate(blocks):
        pieces_ref[i] = block.astype(jnp.bfloat16)


def same_kernel(*refs):
    tiles, (left_ref, left_last_ref, pieces_ref) = refs[:2], refs[2:]
    blocks = lane_products(left_ref[...], left_last_ref[...], tiles, pieces_ref.shape[2])
    for i, block in enumerate(blocks):
        pieces_ref[i] = block


def join_kernel(pieces_ref, other_ref, scale_ref, out_ref):
    blocks = [pieces_ref[i] + other_ref[i].astype(jnp.float32) for i in range(pieces_ref.shape[0])]
    space = out_ref.shape[1] - len(blocks) * blocks[0].shape[1]
    blocks.append(scale_tail(scale_ref[...], blocks[0].shape[0], space))
    out_ref[...] = side_by_side(blocks).astype(out_ref.dtype)


def lanes_image_kernel(own, *refs):
    parts_refs, out_ref = refs[:-1], refs[-1]
    half = len(parts_refs)
    count = parts_refs[0].shape[0]
    total, scales = [0.0] * half, [None] * half
    for m, ref in enumerate(parts_refs):
        part = ref[...].astype(jnp.float32)
        blocks = cut(part[:, : half * own], own)
        for j in range(half):
            total[j] = total[j] + blocks[j ^ m]
        scales[m] = scale_of(part[:, half * own :], own)
    gram, scaled = 0.0, []
    for j in range(half):
        image = total[j] * scales[j]
        gram = gram + lax.dot_general(
            image, image, NT, precision=HIGH, preferred_element_type=jnp.float32
        )
        scaled.append(image * scales[j])
    tail = gram_tail(gram)
    for j in range(half):
        high, low = two_parts(scaled[j])
        here = tail if j == 0 else jnp.zeros_like(tail)
        whole = with_tail(high.astype(jnp.float32), here, out_ref.shape[2])
        out_ref[j, 0:count, :] = whole.astype(jnp.bfloat16)
        whole = with_tail(low.astype(jnp.float32), jnp.zeros_like(tail), out_ref.shape[2])
        out_ref[j, count : 2 * count, :] = whole.astype(jnp.bfloat16)


def row_products(image_ref, tiles, own):
    count = image_ref.shape[1] // 2
    whole = side_by_side([image_ref[i, :, 0:own] for i in range(image_ref.shape[0])])
    values = []
    for refs in (tiles[:-1], tiles[-1:]):
        total = refs[0].shape[0]
        for i in range(0, total, 256):
            value, at = 0.0, 0
            for ref in refs:
                value = value + lax.dot_general(
                    whole[:, at : at + ref.shape[1]], ref[i : min(i + 256, total), :], NT,
                    preferred_element_type=jnp.float32,
                )
                at += ref.shape[1]
            values.append(value[:count] + value[count:])
    return side_by_side(values)


def own_lanes_kernel(own, *refs):
    tiles, (image_ref, out_ref) = refs[:2], refs[2:]
    out_ref[...] = row_products(image_ref, tiles, own)


def other_lanes_kernel(own, *refs):
    tiles, (own_image_ref, image_ref, line_ref), out_refs = refs[:3], refs[3:6], refs[6:]
    count = line_ref.shape[0]
    value = line_ref[...] + row_products(image_ref, tiles, own)
    gram = 0.0
    for ref in (own_image_ref, image_ref):
        gram = gram + gram_of(ref[0, 0:count, :].astype(jnp.float32), own)
    tail = gram_tail(gram)
    for block, ref in zip(cut(value, own), out_refs):
        ref[...] = with_tail(block, tail, ref.shape[1]).astype(ref.dtype)


def eliminate(both, width, block=8):
    count, total = both.shape
    block = math.gcd(count, block)
    repeat = total // 128
    ids = lax.broadcasted_iota(jnp.int32, (count, 128), 0)
    roots = jnp.zeros((count, 128), jnp.float32)

    def wide(value):
        return side_by_side([value] * repeat)

    def down(value):
        return jnp.concatenate([value] * (count // 8), axis=0)

    for k in range(0, count, block):
        columns = [
            jnp.broadcast_to(both[:, width + k + t : width + k + t + 1], (count, 128))
            for t in range(block)
        ]
        corner = {
            (s, t): jnp.broadcast_to(columns[t][k + s : k + s + 1, :], (8, 128))
            for t in range(block)
            for s in range(t, block)
        }
        lines = [
            jnp.broadcast_to(both[k + t : k + t + 1, :], (8, total)) for t in range(block)
        ]
        for t in range(block):
            pivot = corner[t, t]
            inverse = 1.0 / pivot
            roots = jnp.where(ids == k + t, down(1.0 / jnp.sqrt(pivot)), roots)
            lower = {s: corner[s, t] * inverse for s in range(t + 1, block)}
            factor = columns[t] * down(inverse)
            for u in range(t + 1, block):
                columns[u] = columns[u] - factor * down(corner[u, t])
                lines[u] = lines[u] - wide(lower[u]) * lines[t]
                for s in range(u, block):
                    corner[s, u] = corner[s, u] - lower[s] * corner[u, t]
            factor = jnp.where(ids > k + t, factor, 0.0)
            both = both - wide(factor) * down(lines[t])
    return both * wide(roots)


def pack_square(square):
    count = square.shape[0]
    fold = max(1, min(count // 8, 128 // count))
    high = count // fold
    return jnp.concatenate([square[i * high : (i + 1) * high] for i in range(fold)], axis=1)


def unpack_square(packed, count):
    high = packed.shape[0]
    fold = count // high
    return jnp.concatenate(
        [packed[:, i * count : (i + 1) * count] for i in range(fold)], axis=0
    )


def image_kernel(*refs):
    pieces_refs, (scale_ref, image_ref, gram_ref, grams_ref) = refs[:-4], refs[-4:]
    width = scale_ref.shape[1]
    both = sum(ref[...].astype(jnp.float32) for ref in pieces_refs)
    gram_ref[...] = gram_of(both, width)
    image = both[:, :width] * scale_ref[...]
    image_ref[...] = image
    gram = lax.dot_general(image, image, NT, precision=HIGH, preferred_element_type=jnp.float32)
    packed = pack_square(gram)
    for i in range(grams_ref.shape[0]):
        grams_ref[i] = packed


def filled(parts):
    width = sum(p.shape[1] for p in parts)
    space = lanes(width) - width
    if space:
        parts = parts + [jnp.zeros((parts[0].shape[0], space), jnp.float32)]
    return side_by_side(parts)


def middle_kernel(image_ref, gram_ref, out_ref, inverse_ref):
    count, own = image_ref.shape
    rows = lax.broadcasted_iota(jnp.int32, (count, count), 0)
    unit = (rows == lax.broadcasted_iota(jnp.int32, (count, count), 1)).astype(jnp.float32)
    whole = eliminate(filled([image_ref[...], gram_ref[...], unit]), own)
    out_ref[...] = whole[:, :own]
    inverse_ref[...] = whole[:, own + count : own + 2 * count]


def last_kernel(image_ref, inverse_ref, grams_ref, out_ref):
    count, own = image_ref.shape
    inverse = inverse_ref[...]
    gram = unpack_square(jnp.sum(grams_ref[...], axis=0), count)
    gram = jnp.dot(inverse, gram, precision=HIGH, preferred_element_type=jnp.float32)
    gram = lax.dot_general(gram, inverse, NT, precision=HIGH, preferred_element_type=jnp.float32)
    out_ref[...] = eliminate(filled([image_ref[...], gram]), own)[:, :own]


NAMES = ("row_high", "row_low", "col_high", "col_mid", "core")
ROW_SET, LANE_SET = ("row_high", "col_mid"), ("row_low", "col_high", "core")


def swap(value, axes, offset):
    size = lax.axis_size(axes)
    return lax.ppermute(value, axes, [(i, i ^ offset) for i in range(size)])


def stack(first, second):
    half, own = first.shape
    return call(stack_kernel, [((2 * half, own), first.dtype)])(first, second)[0]


def local(embeddings, start_vectors):
    rows, cols = lax.axis_size(ROW_SET), lax.axis_size(LANE_SET)
    own, width = embeddings.shape
    count = start_vectors.shape[0]
    f32, bf16 = jnp.float32, jnp.bfloat16
    half = cols // 2
    even = [*range(0, cols, 2)]
    padded = lanes(own + 1)

    unit, starts = call(own_kernel, [((own, width), bf16), ((count, own), bf16)])(
        embeddings, start_vectors
    )
    row_blocks, lane_blocks = {0: embeddings}, {0: embeddings}
    tops = [m for m in range(1, rows) if m.bit_count() == 1]
    bits = [1 << i for i in range(cols.bit_length() - 2, -1, -1)]
    for m in bits:
        lane_blocks[m] = swap(embeddings, LANE_SET, m)
    unit, lane_blocks[bits[0]] = lax.optimization_barrier((unit, lane_blocks[bits[0]]))
    for m in even:
        if m.bit_count() > 1:
            lane_blocks[m] = swap(lane_blocks[m & (m - 1)], LANE_SET, m & -m)
    first = [(lane_blocks, m, lane_blocks[m]) for m in bits[:0:-1]]
    first += [(row_blocks, m, swap(embeddings, ROW_SET, m)) for m in tops]
    blocks, unit, starts = lax.optimization_barrier(([f[2] for f in first], unit, starts))
    for (where, m, _), block in zip(first, blocks):
        where[m] = block
    for m in even[1:-1]:
        lane_blocks[m + 1] = swap(lane_blocks[m], LANE_SET, 1)
    for m in range(rows):
        if m.bit_count() > 1:
            row_blocks[m] = swap(row_blocks[m & (m - 1)], ROW_SET, m & -m)

    held, here = [0], [starts]
    for m in tops[:0:-1]:
        if len(here) > 1:
            here = [stack(*here)]
        here = [here[0], swap(here[0], ROW_SET, m)]
        held = held + [j ^ m for j in held]

    high, deep = (rows - 1) * own, (half - 1) * own
    unit, farthest = lax.optimization_barrier((unit, lane_blocks[even[-1]]))
    lane_blocks[even[-1]] = farthest
    main_rows, even_lanes, odd_lanes, even_main, odd_main, fold = call(
        functools.partial(main_kernel, rows - 1),
        [
            ((high, width), bf16),
            ((half * own, width), bf16),
            ((deep, width), bf16),
            ((high, half * own), bf16),
            ((high, deep), bf16),
            ((high, 128), f32),
        ],
        flops=2 * high * (half * own + deep) * width,
    )(
        unit,
        *[row_blocks[m] for m in range(1, rows - 1)],
        *[lane_blocks[m] for m in even[1:]],
        *[lane_blocks[m + 1] for m in even[:-1]],
    )
    fold, here[1:], row_blocks[rows - 1] = lax.optimization_barrier(
        (fold, here[1:], row_blocks[rows - 1])
    )
    lines = len(held) * count + -(-2 * rows // 8) * 8
    odd_side, even_last, odd_last, sums, send = call(
        rest_kernel,
        [
            ((high, own), bf16),
            ((own, half * own), bf16),
            ((own, half * own), bf16),
            ((rows, own), f32),
            ((lines, own), bf16),
        ],
        [
            pltpu.VMEM((own, width), bf16),
            pltpu.VMEM((half * own, width), bf16),
            pltpu.VMEM((high, 128), f32),
            pltpu.VMEM((own, 128), f32),
        ],
        flops=2 * (high + cols * own) * own * width,
    )(
        main_rows,
        fold,
        even_lanes,
        odd_lanes,
        row_blocks[rows - 1],
        swap(farthest, LANE_SET, 1),
        *here,
    )
    even_tiles = (even_main, even_last)
    odd_tiles = (odd_main, odd_side, odd_last)

    near = swap(send, ROW_SET, 1)
    sums = [sums] + [swap(sums, ROW_SET, m) for m in range(2, rows)]
    other, left, left_last, degrees, scale = call(
        functools.partial(first_kernel, held, len(here)),
        [
            ((half, count, own), bf16),
            ((count, high), bf16),
            ((count, own), bf16),
            ((1, own), f32),
            ((1, own), f32),
        ],
    )(*odd_tiles, *here, near, *sums)
    other = swap(other, LANE_SET, 1)
    (pieces,) = call(
        same_kernel,
        [((half, count, own), f32)],
        flops=2 * count * rows * half * own * own,
    )(*even_tiles, left, left_last)
    (parts,) = call(join_kernel, [((count, lanes(half * own + 128)), bf16)])(pieces, other, scale)
    parts = [parts] + [swap(parts, LANE_SET, m) for m in even[1:]]

    (image,) = call(functools.partial(lanes_image_kernel, own), [((half, 2 * count, padded), bf16)])(*parts)
    other = swap(image, LANE_SET, 1)
    (value,) = call(
        functools.partial(own_lanes_kernel, own),
        [((count, rows * own), f32)],
        flops=4 * count * rows * half * own * own,
    )(*even_tiles, image)
    wide = lanes(own + 2 * count)
    pieces = call(
        functools.partial(other_lanes_kernel, own),
        [((count, wide), f32 if m == 0 else bf16) for m in range(rows)],
    )(*odd_tiles, image, other, value)
    moved = [swap(pieces[m], ROW_SET, m) for m in range(rows - 1, 0, -1)]
    fold = max(1, min(count // 8, 128 // count))
    image, gram, grams = call(
        image_kernel,
        [
            ((count, own), f32),
            ((count, count), f32),
            ((rows * cols, count // fold, count * fold), f32),
        ],
    )(pieces[0], *moved, scale)
    grams = lax.all_to_all(grams, NAMES, 0, 0, tiled=True)
    image, inverse = call(middle_kernel, [((count, own), f32), ((count, count), f32)])(image, gram)
    (vectors,) = call(last_kernel, [((count, own), f32)])(image, inverse, grams)
    return (vectors, degrees.reshape(own))


def solution(mesh):
    row_size, col_size = mesh.shape["row"], mesh.shape["col"]
    devices = mesh.devices.reshape(row_size // 2, 2, 2, col_size // 4, 2)
    return jax.shard_map(
        local,
        mesh=jax.sharding.Mesh(devices, NAMES),
        in_specs=(P(NAMES, None), P(None, NAMES)),
        out_specs=(P(None, NAMES), P(NAMES)),
        check_vma=False,
    )
```

```python
import functools
import math

import jax
import jax.numpy as jnp
from jax import lax
from jax.experimental import pallas as pl
from jax.experimental.pallas import tpu as pltpu
from jax.sharding import PartitionSpec as P

VMEM = pl.BlockSpec(memory_space=pltpu.VMEM)
NT = (((1,), (1,)), ((), ()))
HIGH = lax.Precision.HIGHEST


def lanes(width):
    return -(-width // 128) * 128


def call(kernel, out_shapes, scratch=(), flops=0):
    count = len(out_shapes)
    mib = 1024 * 1024

    def run(*operands):
        needs = sum(math.prod(o.shape) * jnp.dtype(o.dtype).itemsize for o in operands)
        needs += sum(math.prod(s) * jnp.dtype(d).itemsize for s, d in out_shapes)
        limit = min(56 * mib, 2 * needs // mib * mib + 8 * mib)
        return pl.pallas_call(
            kernel,
            out_shape=[jax.ShapeDtypeStruct(s, d) for s, d in out_shapes],
            in_specs=[VMEM] * len(operands),
            out_specs=[VMEM] * count,
            scratch_shapes=list(scratch),
            compiler_params=pltpu.CompilerParams(vmem_limit_bytes=limit),
            cost_estimate=pl.CostEstimate(flops=flops, bytes_accessed=0, transcendentals=0),
        )(*operands)

    return run


def side_by_side(blocks):
    return jnp.concatenate(blocks, axis=1) if len(blocks) > 1 else blocks[0]


def cut(value, width):
    return [value[:, i : i + width] for i in range(0, value.shape[1], width)]


def two_parts(value):
    high = value.astype(jnp.bfloat16)
    return high, (value - high.astype(jnp.float32)).astype(jnp.bfloat16)


def unit_rows(ref, gain):
    values = ref[...].astype(jnp.float32)
    power = jnp.mean(values * values, axis=1, keepdims=True)
    factor = lax.rsqrt(power + 1e-06) * (gain / math.sqrt(ref.shape[1]))
    return (values * factor).astype(jnp.bfloat16)


def own_kernel(emb_ref, start_ref, unit_ref, out_ref):
    unit_ref[...] = unit_rows(emb_ref, 1.0)
    out_ref[...] = start_ref[...].astype(out_ref.dtype)


def stack_kernel(first_ref, second_ref, out_ref):
    half = first_ref.shape[0]
    out_ref[0:half, :] = first_ref[...]
    out_ref[half : 2 * half, :] = second_ref[...]


def affinity(rows_ref, parts, own, fold_ref, more_ref=None):
    def row_block(start):
        piece = rows_ref[pl.ds(start, own), :]
        fold = 0.0 if more_ref is None else more_ref[pl.ds(start, own), :]
        for lanes_ref, first, tile_ref in parts:
            total = tile_ref.shape[1]
            for j in range(0, total, 256):
                stop = min(j + 256, total)
                inner = lax.dot_general(
                    piece, lanes_ref[first + j : first + stop, :], NT,
                    preferred_element_type=jnp.float32,
                )
                values = jnp.exp(inner - 8.0)
                tile_ref[pl.ds(start, own), j:stop] = values.astype(jnp.bfloat16)
                for part in cut(values, 128):
                    gap = 128 - part.shape[1]
                    if gap:
                        part = side_by_side([part, jnp.zeros((own, gap), jnp.float32)])
                    fold = fold + part
        fold_ref[pl.ds(start, own), :] = fold

    count = rows_ref.shape[0] // own
    if count <= 4:
        for i in range(count):
            row_block(i * own)
    else:
        pl.loop(0, count)(lambda i: row_block(pl.multiple_of(i * own, own)))


def unfold(fold):
    ones = jnp.ones((8, fold.shape[1]), jnp.float32)
    sums = lax.dot_general(ones, fold, NT, precision=HIGH, preferred_element_type=jnp.float32)
    return sums[0:1, :]


def main_kernel(rows, unit_ref, *refs):
    row_refs, lane_refs = refs[: rows - 1], refs[rows - 1 : -6]
    rows_ref, even_ref, odd_ref, even_tile_ref, odd_tile_ref, fold_ref = refs[-6:]
    own = unit_ref.shape[0]
    rows_ref[0:own, :] = unit_ref[...] * 8
    even_ref[0:own, :] = unit_ref[...]
    for i, ref in enumerate(row_refs, 1):
        rows_ref[i * own : (i + 1) * own, :] = unit_rows(ref, 8.0)
    half = even_ref.shape[0] // own
    for i, ref in enumerate(lane_refs, 1):
        target, at = (even_ref, i) if i < half else (odd_ref, i - half)
        target[at * own : (at + 1) * own, :] = unit_rows(ref, 1.0)
    parts = [(even_ref, 0, even_tile_ref), (odd_ref, 0, odd_tile_ref)]
    affinity(rows_ref, parts, own, fold_ref)


def rest_kernel(rows_ref, fold_in_ref, even_ref, odd_in_ref, row_ref, fresh_ref, *refs):
    start_refs, refs = refs[:-9], refs[-9:]
    side_tile_ref, even_last_ref, odd_last_ref, sums_ref, send_ref = refs[:5]
    last_ref, odd_ref, fold_ref, fold_last_ref = refs[5:]
    own = row_ref.shape[0]
    high = odd_in_ref.shape[0]
    odd_ref[0:high, :] = odd_in_ref[...]
    odd_ref[high : high + own, :] = unit_rows(fresh_ref, 1.0)
    affinity(rows_ref, [(odd_ref, high, side_tile_ref)], own, fold_ref, fold_in_ref)
    last_ref[...] = unit_rows(row_ref, 8.0)
    parts = [(even_ref, 0, even_last_ref), (odd_ref, 0, odd_last_ref)]
    affinity(last_ref, parts, own, fold_last_ref)
    lines = cut(unfold(fold_ref[...]), own) + [unfold(fold_last_ref[...])]
    sums = jnp.concatenate(lines, axis=0)
    sums_ref[...] = sums
    parts = [ref[...].astype(jnp.float32) for ref in start_refs]
    parts += [part.astype(jnp.float32) for part in two_parts(sums)]
    space = send_ref.shape[0] - sum(p.shape[0] for p in parts)
    if space:
        parts.append(jnp.zeros((space, own), jnp.float32))
    send_ref[...] = jnp.concatenate(parts, axis=0).astype(jnp.bfloat16)


def lane_products(left, last, tiles, own):
    def product(value, ref):
        return side_by_side(
            [
                jnp.dot(value, ref[:, i : i + 256], preferred_element_type=jnp.float32)
                for i in range(0, ref.shape[1], 256)
            ]
        )

    blocks = [block for ref in tiles[:-1] for block in cut(product(left, ref), own)]
    return [x + y for x, y in zip(blocks, cut(product(last, tiles[-1]), own))]


def with_tail(block, tail, width):
    space = width - block.shape[1] - tail.shape[1]
    parts = [block, tail]
    if space:
        parts.append(jnp.zeros((block.shape[0], space), jnp.float32))
    return side_by_side(parts)


def gram_tail(gram):
    return side_by_side([p.astype(jnp.float32) for p in two_parts(gram)])


def gram_of(piece, own):
    count = piece.shape[0]
    return piece[:, own : own + count] + piece[:, own + count : own + 2 * count]


def scale_tail(scale, count, space):
    lines = []
    for part in two_parts(scale):
        for piece in cut(part.astype(jnp.float32), space):
            gap = space - piece.shape[1]
            lines.append(side_by_side([piece, jnp.zeros((1, gap), jnp.float32)]) if gap else piece)
    lines.append(jnp.zeros((count - len(lines), space), jnp.float32))
    return jnp.concatenate(lines, axis=0)


def scale_of(tail, own):
    lines = -(-own // tail.shape[1])
    parts = [
        side_by_side([tail[k + i : k + i + 1] for i in range(lines)])[:, :own]
        for k in (0, lines)
    ]
    return parts[0] + parts[1]


def first_kernel(held, steps, *refs):
    tiles, start_refs = refs[:3], refs[3 : 3 + steps]
    near_ref, sums_refs = refs[3 + steps], refs[4 + steps : -5]
    pieces_ref, left_ref, left_last_ref, degrees_ref, scale_ref = refs[-5:]
    rows, own = sums_refs[0].shape
    count = pieces_ref.shape[1]
    near = near_ref[...].astype(jnp.float32)
    here = len(held) * count
    sums = [ref[...] for ref in sums_refs]
    sums.insert(1, near[here : here + rows] + near[here + rows : here + 2 * rows])
    blocks = [ref[...].astype(jnp.float32) for ref in start_refs] + [near[:here]]
    blocks = [b[i : i + count] for b in blocks for i in range(0, b.shape[0], count)]
    places = held + [m ^ 1 for m in held]
    starts = [blocks[places.index(j)] for j in range(rows)]
    degrees = []
    for j in range(rows):
        degrees.append(sum(s[j ^ m : (j ^ m) + 1, :] for m, s in enumerate(sums)))
    degrees_ref[...] = degrees[0]
    scales = [1.0 / jnp.sqrt(d) for d in degrees]
    scale_ref[...] = scales[0]
    scaled = [(start * scale).astype(jnp.bfloat16) for start, scale in zip(starts, scales)]
    left_ref[...] = side_by_side(scaled[:-1])
    left_last_ref[...] = scaled[-1]
    blocks = lane_products(left_ref[...], left_last_ref[...], tiles, own)
    for i, block in enumerate(blocks):
        pieces_ref[i] = block.astype(jnp.bfloat16)


def same_kernel(*refs):
    tiles, (left_ref, left_last_ref, pieces_ref) = refs[:2], refs[2:]
    blocks = lane_products(left_ref[...], left_last_ref[...], tiles, pieces_ref.shape[2])
    for i, block in enumerate(blocks):
        pieces_ref[i] = block


def join_kernel(pieces_ref, other_ref, scale_ref, out_ref):
    blocks = [pieces_ref[i] + other_ref[i].astype(jnp.float32) for i in range(pieces_ref.shape[0])]
    space = out_ref.shape[1] - len(blocks) * blocks[0].shape[1]
    blocks.append(scale_tail(scale_ref[...], blocks[0].shape[0], space))
    out_ref[...] = side_by_side(blocks).astype(out_ref.dtype)


def lanes_image_kernel(own, *refs):
    parts_refs, out_ref = refs[:-1], refs[-1]
    half = len(parts_refs)
    count = parts_refs[0].shape[0]
    total, scales = [0.0] * half, [None] * half
    for m, ref in enumerate(parts_refs):
        part = ref[...].astype(jnp.float32)
        blocks = cut(part[:, : half * own], own)
        for j in range(half):
            total[j] = total[j] + blocks[j ^ m]
        scales[m] = scale_of(part[:, half * own :], own)
    gram, scaled = 0.0, []
    for j in range(half):
        image = total[j] * scales[j]
        gram = gram + lax.dot_general(
            image, image, NT, precision=HIGH, preferred_element_type=jnp.float32
        )
        scaled.append(image * scales[j])
    tail = gram_tail(gram)
    for j in range(half):
        high, low = two_parts(scaled[j])
        here = tail if j == 0 else jnp.zeros_like(tail)
        whole = with_tail(high.astype(jnp.float32), here, out_ref.shape[2])
        out_ref[j, 0:count, :] = whole.astype(jnp.bfloat16)
        whole = with_tail(low.astype(jnp.float32), jnp.zeros_like(tail), out_ref.shape[2])
        out_ref[j, count : 2 * count, :] = whole.astype(jnp.bfloat16)


def row_products(image_ref, tiles, own):
    count = image_ref.shape[1] // 2
    whole = side_by_side([image_ref[i, :, 0:own] for i in range(image_ref.shape[0])])
    values = []
    for refs in (tiles[:-1], tiles[-1:]):
        total = refs[0].shape[0]
        for i in range(0, total, 256):
            value, at = 0.0, 0
            for ref in refs:
                value = value + lax.dot_general(
                    whole[:, at : at + ref.shape[1]], ref[i : min(i + 256, total), :], NT,
                    preferred_element_type=jnp.float32,
                )
                at += ref.shape[1]
            values.append(value[:count] + value[count:])
    return side_by_side(values)


def own_lanes_kernel(own, *refs):
    tiles, (image_ref, out_ref) = refs[:2], refs[2:]
    out_ref[...] = row_products(image_ref, tiles, own)


def other_lanes_kernel(own, *refs):
    tiles, (own_image_ref, image_ref, line_ref), out_refs = refs[:3], refs[3:6], refs[6:]
    count = line_ref.shape[0]
    value = line_ref[...] + row_products(image_ref, tiles, own)
    gram = 0.0
    for ref in (own_image_ref, image_ref):
        gram = gram + gram_of(ref[0, 0:count, :].astype(jnp.float32), own)
    tail = gram_tail(gram)
    for block, ref in zip(cut(value, own), out_refs):
        ref[...] = with_tail(block, tail, ref.shape[1]).astype(ref.dtype)


def eliminate(both, width, block=8):
    count, total = both.shape
    block = math.gcd(count, block)
    repeat = total // 128
    ids = lax.broadcasted_iota(jnp.int32, (count, 128), 0)
    roots = jnp.zeros((count, 128), jnp.float32)

    def wide(value):
        return side_by_side([value] * repeat)

    def down(value):
        return jnp.concatenate([value] * (count // 8), axis=0)

    for k in range(0, count, block):
        columns = [
            jnp.broadcast_to(both[:, width + k + t : width + k + t + 1], (count, 128))
            for t in range(block)
        ]
        corner = {
            (s, t): jnp.broadcast_to(columns[t][k + s : k + s + 1, :], (8, 128))
            for t in range(block)
            for s in range(t, block)
        }
        lines = [
            jnp.broadcast_to(both[k + t : k + t + 1, :], (8, total)) for t in range(block)
        ]
        for t in range(block):
            pivot = corner[t, t]
            inverse = 1.0 / pivot
            roots = jnp.where(ids == k + t, down(1.0 / jnp.sqrt(pivot)), roots)
            lower = {s: corner[s, t] * inverse for s in range(t + 1, block)}
            factor = columns[t] * down(inverse)
            for u in range(t + 1, block):
                columns[u] = columns[u] - factor * down(corner[u, t])
                lines[u] = lines[u] - wide(lower[u]) * lines[t]
                for s in range(u, block):
                    corner[s, u] = corner[s, u] - lower[s] * corner[u, t]
            factor = jnp.where(ids > k + t, factor, 0.0)
            both = both - wide(factor) * down(lines[t])
    return both * wide(roots)


def pack_square(square):
    count = square.shape[0]
    fold = max(1, min(count // 8, 128 // count))
    high = count // fold
    return jnp.concatenate([square[i * high : (i + 1) * high] for i in range(fold)], axis=1)


def unpack_square(packed, count):
    high = packed.shape[0]
    fold = count // high
    return jnp.concatenate(
        [packed[:, i * count : (i + 1) * count] for i in range(fold)], axis=0
    )


def image_kernel(*refs):
    pieces_refs, (scale_ref, image_ref, gram_ref, grams_ref) = refs[:-4], refs[-4:]
    width = scale_ref.shape[1]
    both = sum(ref[...].astype(jnp.float32) for ref in pieces_refs)
    gram_ref[...] = gram_of(both, width)
    image = both[:, :width] * scale_ref[...]
    image_ref[...] = image
    gram = lax.dot_general(image, image, NT, precision=HIGH, preferred_element_type=jnp.float32)
    packed = pack_square(gram)
    for i in range(grams_ref.shape[0]):
        grams_ref[i] = packed


def filled(parts):
    width = sum(p.shape[1] for p in parts)
    space = lanes(width) - width
    if space:
        parts = parts + [jnp.zeros((parts[0].shape[0], space), jnp.float32)]
    return side_by_side(parts)


def middle_kernel(image_ref, gram_ref, out_ref, inverse_ref):
    count, own = image_ref.shape
    rows = lax.broadcasted_iota(jnp.int32, (count, count), 0)
    unit = (rows == lax.broadcasted_iota(jnp.int32, (count, count), 1)).astype(jnp.float32)
    whole = eliminate(filled([image_ref[...], gram_ref[...], unit]), own)
    out_ref[...] = whole[:, :own]
    inverse_ref[...] = whole[:, own + count : own + 2 * count]


def last_kernel(image_ref, inverse_ref, grams_ref, out_ref):
    count, own = image_ref.shape
    inverse = inverse_ref[...]
    gram = unpack_square(jnp.sum(grams_ref[...], axis=0), count)
    gram = jnp.dot(inverse, gram, precision=HIGH, preferred_element_type=jnp.float32)
    gram = lax.dot_general(gram, inverse, NT, precision=HIGH, preferred_element_type=jnp.float32)
    out_ref[...] = eliminate(filled([image_ref[...], gram]), own)[:, :own]


NAMES = ("row_high", "row_low", "col_high", "col_mid", "core")
ROW_SET, LANE_SET = ("row_high", "col_mid"), ("row_low", "col_high", "core")


def swap(value, axes, offset):
    size = lax.axis_size(axes)
    return lax.ppermute(value, axes, [(i, i ^ offset) for i in range(size)])


def stack(first, second):
    half, own = first.shape
    return call(stack_kernel, [((2 * half, own), first.dtype)])(first, second)[0]


def local(embeddings, start_vectors):
    rows, cols = lax.axis_size(ROW_SET), lax.axis_size(LANE_SET)
    own, width = embeddings.shape
    count = start_vectors.shape[0]
    f32, bf16 = jnp.float32, jnp.bfloat16
    half = cols // 2
    even = [*range(0, cols, 2)]
    padded = lanes(own + 1)

    unit, starts = call(own_kernel, [((own, width), bf16), ((count, own), bf16)])(
        embeddings, start_vectors
    )
    row_blocks, lane_blocks = {0: embeddings}, {0: embeddings}
    tops = [m for m in range(1, rows) if m.bit_count() == 1]
    bits = [1 << i for i in range(cols.bit_length() - 2, -1, -1)]
    for m in bits:
        lane_blocks[m] = swap(embeddings, LANE_SET, m)
    unit, lane_blocks[bits[0]] = lax.optimization_barrier((unit, lane_blocks[bits[0]]))
    for m in even:
        if m.bit_count() > 1:
            lane_blocks[m] = swap(lane_blocks[m & (m - 1)], LANE_SET, m & -m)
    first = [(lane_blocks, m, lane_blocks[m]) for m in bits[:0:-1]]
    first += [(row_blocks, m, swap(embeddings, ROW_SET, m)) for m in tops]
    blocks, unit, starts = lax.optimization_barrier(([f[2] for f in first], unit, starts))
    for (where, m, _), block in zip(first, blocks):
        where[m] = block
    for m in even[1:-1]:
        lane_blocks[m + 1] = swap(lane_blocks[m], LANE_SET, 1)
    for m in range(rows):
        if m.bit_count() > 1:
            row_blocks[m] = swap(row_blocks[m & (m - 1)], ROW_SET, m & -m)

    held, here = [0], [starts]
    for m in tops[:0:-1]:
        if len(here) > 1:
            here = [stack(*here)]
        here = [here[0], swap(here[0], ROW_SET, m)]
        held = held + [j ^ m for j in held]

    high, deep = (rows - 1) * own, (half - 1) * own
    unit, here[1:], farthest = lax.optimization_barrier((unit, here[1:], lane_blocks[even[-1]]))
    lane_blocks[even[-1]] = farthest
    main_rows, even_lanes, odd_lanes, even_main, odd_main, fold = call(
        functools.partial(main_kernel, rows - 1),
        [
            ((high, width), bf16),
            ((half * own, width), bf16),
            ((deep, width), bf16),
            ((high, half * own), bf16),
            ((high, deep), bf16),
            ((high, 128), f32),
        ],
        flops=2 * high * (half * own + deep) * width,
    )(
        unit,
        *[row_blocks[m] for m in range(1, rows - 1)],
        *[lane_blocks[m] for m in even[1:]],
        *[lane_blocks[m + 1] for m in even[:-1]],
    )
    lines = len(held) * count + -(-2 * rows // 8) * 8
    odd_side, even_last, odd_last, sums, send = call(
        rest_kernel,
        [
            ((high, own), bf16),
            ((own, half * own), bf16),
            ((own, half * own), bf16),
            ((rows, own), f32),
            ((lines, own), bf16),
        ],
        [
            pltpu.VMEM((own, width), bf16),
            pltpu.VMEM((half * own, width), bf16),
            pltpu.VMEM((high, 128), f32),
            pltpu.VMEM((own, 128), f32),
        ],
        flops=2 * (high + cols * own) * own * width,
    )(
        main_rows,
        fold,
        even_lanes,
        odd_lanes,
        row_blocks[rows - 1],
        swap(farthest, LANE_SET, 1),
        *here,
    )
    even_tiles = (even_main, even_last)
    odd_tiles = (odd_main, odd_side, odd_last)

    near = swap(send, ROW_SET, 1)
    sums = [sums] + [swap(sums, ROW_SET, m) for m in range(2, rows)]
    other, left, left_last, degrees, scale = call(
        functools.partial(first_kernel, held, len(here)),
        [
            ((half, count, own), bf16),
            ((count, high), bf16),
            ((count, own), bf16),
            ((1, own), f32),
            ((1, own), f32),
        ],
    )(*odd_tiles, *here, near, *sums)
    other = swap(other, LANE_SET, 1)
    (pieces,) = call(
        same_kernel,
        [((half, count, own), f32)],
        flops=2 * count * rows * half * own * own,
    )(*even_tiles, left, left_last)
    (parts,) = call(join_kernel, [((count, lanes(half * own + 128)), bf16)])(pieces, other, scale)
    parts = [parts] + [swap(parts, LANE_SET, m) for m in even[1:]]

    (image,) = call(functools.partial(lanes_image_kernel, own), [((half, 2 * count, padded), bf16)])(*parts)
    other = swap(image, LANE_SET, 1)
    (value,) = call(
        functools.partial(own_lanes_kernel, own),
        [((count, rows * own), f32)],
        flops=4 * count * rows * half * own * own,
    )(*even_tiles, image)
    wide = lanes(own + 2 * count)
    pieces = call(
        functools.partial(other_lanes_kernel, own),
        [((count, wide), f32 if m == 0 else bf16) for m in range(rows)],
    )(*odd_tiles, image, other, value)
    moved = [swap(pieces[m], ROW_SET, m) for m in range(rows - 1, 0, -1)]
    fold = max(1, min(count // 8, 128 // count))
    image, gram, grams = call(
        image_kernel,
        [
            ((count, own), f32),
            ((count, count), f32),
            ((rows * cols, count // fold, count * fold), f32),
        ],
    )(pieces[0], *moved, scale)
    grams = lax.all_to_all(grams, NAMES, 0, 0, tiled=True)
    image, inverse = call(middle_kernel, [((count, own), f32), ((count, count), f32)])(image, gram)
    (vectors,) = call(last_kernel, [((count, own), f32)])(image, inverse, grams)
    return (vectors, degrees.reshape(own))


def solution(mesh):
    row_size, col_size = mesh.shape["row"], mesh.shape["col"]
    devices = mesh.devices.reshape(row_size // 2, 2, 2, col_size // 4, 2)
    return jax.shard_map(
        local,
        mesh=jax.sharding.Mesh(devices, NAMES),
        in_specs=(P(NAMES, None), P(None, NAMES)),
        out_specs=(P(None, NAMES), P(NAMES)),
        check_vma=False,
    )
```
